32 devices in a mesh: rows: 4 (over x, core), hidden: 8 (over z, y).
Axes of the slice: x: 2, y: 2, z: 4, core: 2. Of those that a mesh axis runs over, the one named last changes fastest.
Arguments:
- resid_stream: bfloat16 [1024, 3584], P('rows'), may hold values from -6 to 6
- pre_gain: float32 [3584], replicated, may hold values from -0.5 to 0.5
- w_gate: bfloat16 [3584, 14336], P(None, 'hidden'), may hold values from -0.09375 to 0.09375
- w_up: bfloat16 [3584, 14336], P(None, 'hidden'), may hold values from -0.09375 to 0.09375
- w_down: bfloat16 [14336, 3584], P('hidden'), may hold values from -0.0625 to 0.0625
- w_enc: bfloat16 [3584, 8192], P(None, ('rows', 'hidden')), may hold values from -0.09375 to 0.09375
- b_enc: bfloat16 [8192], P(('rows', 'hidden')), may hold values from -3 to 3
- w_dec: bfloat16 [8192, 3584], P(('rows', 'hidden')), may hold values from -0.0625 to 0.0625
- b_dec: float32 [3584], replicated, may hold values from -3 to 3
Outputs:
- enc_grad: float32 [3584, 8192], P(None, ('rows', 'hidden'))
- dec_grad: float32 [8192, 3584], P(('rows', 'hidden'))
The draws below stay inside these ranges and needn't reach their ends.
All inputs are finite; a program needn't handle non-finite values.
Results may differ from the reference program's by a relative error of at most 0.0062.
Values may be sent and summed in bfloat16 or wider, within the bound.
A program may use at most 128 MiB of HBM per device.

```python
import jax
import jax.numpy as jnp
from jax import lax

D = 3584
FF = 14336
TOKENS = 1024
LAT = 8192


def strengthened(values, stream_key, source, target, shards_of, factor):
    def block_of(axis_at):
        return (jnp.arange(values.shape[axis_at]) // (values.shape[axis_at] // shards_of)).reshape((-1,) + (1,) * (values.ndim - 1 - axis_at))

    near = jax.random.permutation(stream_key, shards_of)[block_of(target)]
    far = (block_of(target) + shards_of // 2) % shards_of
    return jnp.where((block_of(source) == near) | (block_of(source) == far), factor * values, values)


def shard_levels(stream_key, shape, pieces, least, largest):
    level = 1.0
    for position, shards_of in pieces:
        heights = jax.random.uniform(jax.random.fold_in(jax.random.fold_in(stream_key, 6), position), (shards_of,), jnp.float32, least / len(pieces), largest / len(pieces))
        level = level * jnp.repeat(jnp.exp(heights), shape[position] // shards_of).reshape((-1,) + (1,) * (len(shape) - 1 - position))
    return level


def bell_draw(key, dims, width, limit, shards=(), kind=jnp.bfloat16):
    gain = shard_levels(key, dims, shards, -0.22, 0.18) if shards else 1.0
    array = jax.random.normal(key, dims, jnp.float32) * width * gain
    return jnp.minimum(jnp.maximum(array, -limit), limit).astype(kind)


def noise_with(rng, extent, deviation, most, pieces, heavy, kind=jnp.bfloat16):
    drawn = deviation * jax.random.normal(rng, extent, jnp.float32)
    if pieces:
        drawn = drawn * shard_levels(rng, extent, pieces, -0.22, 0.18)
    return jnp.clip(strengthened(drawn, jax.random.fold_in(rng, 3), *heavy), -most, most).astype(kind)


def setup_inputs(seed: int = 0) -> dict:
    seeds = jax.random.split(jax.random.key(seed), 10)
    return {
        "resid_stream": bell_draw(seeds[0], (TOKENS, D), 1.0, 6.0, ((0, 4),)),
        "pre_gain": jnp.clip(jax.random.uniform(seeds[1], (D,), jnp.float32, -0.5, 0.5), -0.5, 0.5),
        "w_gate": bell_draw(seeds[2], (D, FF), D ** -0.5, 0.09375, ((1, 8),)),
        "w_up": bell_draw(seeds[3], (D, FF), D ** -0.5, 0.09375, ((1, 8),)),
        "w_down": noise_with(seeds[4], (FF, D), FF ** -0.5, 0.0625, ((0, 8),), (0, 1, 8, 2.0)),
        "w_enc": bell_draw(seeds[5], (D, LAT), D ** -0.5, 0.09375, ((1, 32),)),
        "b_enc": bell_draw(seeds[6], (LAT,), 0.5, 3.0, ((0, 32),)),
        "w_dec": bell_draw(seeds[7], (LAT, D), LAT ** -0.5, 0.0625, ((0, 32),)),
        "b_dec": bell_draw(seeds[8], (D,), 0.5, 3.0, (), jnp.float32),
    }


def reference(resid_stream, pre_gain, w_gate, w_up, w_down, w_enc, b_enc, w_dec, b_dec):
    values = resid_stream.astype(jnp.float32)
    variance = lax.optimization_barrier(jnp.mean(values * values, axis=-1, keepdims=True))
    normal_in = (values * lax.rsqrt(variance + 1e-06) * (1.0 + pre_gain)).astype(jnp.bfloat16)
    gate_proj = jnp.dot(normal_in, w_gate, preferred_element_type=jnp.float32)
    up_proj = jnp.dot(normal_in, w_up, preferred_element_type=jnp.float32)
    hidden_units = (jax.nn.gelu(gate_proj, approximate=True) * up_proj).astype(jnp.bfloat16)
    target = jnp.dot(hidden_units, w_down, preferred_element_type=jnp.float32)
    pre_act = jnp.dot(normal_in, w_enc, preferred_element_type=jnp.float32) + b_enc.astype(jnp.float32)
    rectified = jnp.maximum(pre_act, 0.0)
    latent = (rectified * rectified).astype(jnp.bfloat16)
    recon = jnp.dot(latent, w_dec, preferred_element_type=jnp.float32) + b_dec
    misfit = (recon - target).astype(jnp.bfloat16)
    factor = 1.0 / TOKENS ** 0.5
    dec_grad = lax.dot_general(latent, misfit, (((0,), (0,)), ((), ())), preferred_element_type=jnp.float32) * factor
    back_prop = lax.dot_general(misfit, w_dec, (((1,), (1,)), ((), ())), preferred_element_type=jnp.float32)
    slope = (back_prop * 2.0 * rectified).astype(jnp.bfloat16)
    enc_grad = lax.dot_general(normal_in, slope, (((0,), (0,)), ((), ())), preferred_element_type=jnp.float32) * factor
    return (enc_grad, dec_grad)
```

```python
import functools
import math

import jax
import jax.numpy as jnp
from jax import lax
from jax.experimental import pallas as pl
from jax.experimental.pallas import tpu as pltpu
from jax.sharding import PartitionSpec as P

LANES = 128


def normed(resid_stream, pre_gain):
    values = resid_stream.astype(jnp.float32)
    variance = jnp.mean(values * values, axis=-1, keepdims=True)
    return (values * lax.rsqrt(variance + 1e-06) * (1.0 + pre_gain)).astype(jnp.bfloat16)


def contract_first(left, right):
    return lax.dot_general(
        left, right, (((0,), (0,)), ((), ())), preferred_element_type=jnp.float32
    )


def contract_last(left, right):
    return lax.dot_general(
        left, right, (((1,), (1,)), ((), ())), preferred_element_type=jnp.float32
    )


def by_rows(count, block, body):
    def step(i, carry):
        body(pl.multiple_of(i * block, block))
        return carry

    lax.fori_loop(0, count // block, step, 0)


def groups_of(half, count=4):
    tiles = half // LANES
    out, at = [], 0
    for i in range(count):
        width = (tiles // count + (1 if i < tiles % count else 0)) * LANES
        out.append((at, width))
        at += width
    return out


def total_kernel(
    z_size, part_ref, bias_ref, out_ref,
    core_in, acc0, in1, acc1, in2, acc2, in3, send_sem, recv_sem,
):
    tokens, features = part_ref.shape
    half_f = features // 2
    groups = groups_of(half_f)
    row, hid = lax.axis_index("rows"), lax.axis_index("hidden")
    x, core = row // 2, row % 2
    z, y = hid // 2, hid % 2
    core_peer = {"rows": x * 2 + (1 - core), "hidden": hid}
    x_peer = {"rows": (1 - x) * 2 + core, "hidden": hid}
    y_peer = {"rows": row, "hidden": z * 2 + (1 - y)}
    z_peers = [
        {"rows": row, "hidden": lax.rem(z + d, z_size) * 2 + y} for d in range(1, z_size)
    ]
    stages = 2 * (3 + z_size - 1)

    barrier = pltpu.get_barrier_semaphore()
    peers = [core_peer, x_peer, y_peer] + z_peers
    for peer in peers:
        pl.semaphore_signal(barrier, inc=1, device_id=peer, device_id_type=pl.DeviceIdType.MESH)
    pl.semaphore_wait(barrier, len(peers))

    def copy(group, stage, src, dst, peer):
        at = group * stages + stage
        return pltpu.make_async_remote_copy(
            src_ref=src, dst_ref=dst, send_sem=send_sem.at[at], recv_sem=recv_sem.at[at],
            device_id=peer, device_id_type=pl.DeviceIdType.MESH,
        )

    t1, t2, t3 = tokens // 2, tokens // 4, tokens // (4 * z_size)
    started = []

    def go(copies):
        for c in copies:
            c.start()
        started.extend(copies)
        return copies

    def mine(off, width):
        return pl.ds(pl.multiple_of(core * half_f + off, LANES), width)

    def rows_at(start, size):
        return pl.ds(pl.multiple_of(start, size), size)

    def bits(g):
        return (x, y, x_peer, y_peer) if g % 2 == 0 else (y, x, y_peer, x_peer)

    flying = []
    for g, (off, width) in enumerate(groups):
        theirs = pl.ds(pl.multiple_of((1 - core) * half_f + off, LANES), width)
        flying.append(go([copy(g, 0, part_ref.at[:, theirs], core_in.at[:, pl.ds(off, width)], core_peer)]))

    for g, (off, width) in enumerate(groups):
        b1, b2, p1, p2 = bits(g)
        cols, own = pl.ds(off, width), mine(off, width)
        flying[g][0].wait_recv()

        def add0(i):
            rows = pl.ds(i, 32)
            acc0[rows, cols] = (
                part_ref[rows, own].astype(jnp.float32) + core_in[rows, cols].astype(jnp.float32)
            ).astype(jnp.bfloat16)

        by_rows(tokens, 32, add0)
        flying[g] = go([copy(g, 1, acc0.at[rows_at((1 - b1) * t1, t1), cols], in1.at[:, cols], p1)])

    for g, (off, width) in enumerate(groups):
        b1, b2, p1, p2 = bits(g)
        cols = pl.ds(off, width)
        flying[g][0].wait_recv()

        def add1(i):
            rows = pl.ds(i, 32)
            kept = pl.ds(pl.multiple_of(b1 * t1 + i, 32), 32)
            acc1[rows, cols] = (
                acc0[kept, cols].astype(jnp.float32) + in1[rows, cols].astype(jnp.float32)
            ).astype(jnp.bfloat16)

        by_rows(t1, 32, add1)
        flying[g] = go([copy(g, 2, acc1.at[rows_at((1 - b2) * t2, t2), cols], in2.at[:, cols], p2)])

    for g, (off, width) in enumerate(groups):
        b1, b2, p1, p2 = bits(g)
        cols = pl.ds(off, width)
        flying[g][0].wait_recv()

        def add2(i):
            rows = pl.ds(i, 32)
            kept = pl.ds(pl.multiple_of(b2 * t2 + i, 32), 32)
            acc2[rows, cols] = (
                acc1[kept, cols].astype(jnp.float32) + in2[rows, cols].astype(jnp.float32)
            ).astype(jnp.bfloat16)

        by_rows(t2, 32, add2)
        flying[g] = go([
            copy(g, 3 + d, acc2.at[rows_at(lax.rem(z + 1 + d, z_size) * t3, t3), cols],
                 in3.at[d, :, cols], z_peers[d])
            for d in range(z_size - 1)
        ])

    base = 3 + z_size - 1
    for g, (off, width) in enumerate(groups):
        b1, b2, p1, p2 = bits(g)
        cols, own = pl.ds(off, width), mine(off, width)
        for c in flying[g]:
            c.wait_recv()
        start = b1 * t1 + b2 * t2 + z * t3

        def add3(i):
            rows = pl.ds(i, 16)
            total = acc2[pl.ds(pl.multiple_of(z * t3 + i, 16), 16), cols].astype(jnp.float32)
            for d in range(z_size - 1):
                total = total + in3[d, rows, cols].astype(jnp.float32)
            total = total + bias_ref[:, own]
            out_ref[pl.ds(pl.multiple_of(start + i, 16), 16), own] = total.astype(jnp.bfloat16)

        by_rows(t3, 16, add3)
        block = out_ref.at[rows_at(start, t3), own]
        flying[g] = go([copy(g, base + d, block, block, z_peers[d]) for d in range(z_size - 1)])

    for g, (off, width) in enumerate(groups):
        b1, b2, p1, p2 = bits(g)
        for c in flying[g]:
            c.wait_recv()
        block = out_ref.at[rows_at(b1 * t1 + b2 * t2, t2), mine(off, width)]
        flying[g] = go([copy(g, base + z_size - 1, block, block, p2)])

    for g, (off, width) in enumerate(groups):
        b1, b2, p1, p2 = bits(g)
        flying[g][0].wait_recv()
        block = out_ref.at[rows_at(b1 * t1, t1), mine(off, width)]
        flying[g] = go([copy(g, base + z_size, block, block, p1)])

    for g, (off, width) in enumerate(groups):
        flying[g][0].wait_recv()
        block = out_ref.at[:, mine(off, width)]
        flying[g] = go([copy(g, base + z_size + 1, block, block, core_peer)])

    for g in range(len(groups)):
        flying[g][0].wait_recv()
    for c in started:
        c.wait_send()


def total_over_devices(part, bias, z_size):
    tokens, features = part.shape
    half_f = features // 2
    stages = 2 * (3 + z_size - 1) * len(groups_of(half_f))
    t1, t2, t3 = tokens // 2, tokens // 4, tokens // (4 * z_size)
    bf = jnp.bfloat16
    return pl.pallas_call(
        functools.partial(total_kernel, z_size),
        out_shape=jax.ShapeDtypeStruct((tokens, features), bf),
        in_specs=[pl.BlockSpec(memory_space=pltpu.VMEM)] * 2,
        out_specs=pl.BlockSpec(memory_space=pltpu.VMEM),
        scratch_shapes=[
            pltpu.VMEM((tokens, half_f), bf),
            pltpu.VMEM((tokens, half_f), bf),
            pltpu.VMEM((t1, half_f), bf),
            pltpu.VMEM((t1, half_f), bf),
            pltpu.VMEM((t2, half_f), bf),
            pltpu.VMEM((t2, half_f), bf),
            pltpu.VMEM((z_size - 1, t3, half_f), bf),
            pltpu.SemaphoreType.DMA((stages,)),
            pltpu.SemaphoreType.DMA((stages,)),
        ],
        compiler_params=pltpu.CompilerParams(
            collective_id=0, has_side_effects=True, vmem_limit_bytes=48 * 1024 * 1024
        ),
    )(part, bias)


def on_device(z_size, resid_stream, pre_gain, w_gate, w_up, w_down, w_enc, b_enc, w_dec, b_dec):
    normal_in = normed(resid_stream, pre_gain)
    tok_rows = lax.all_gather(normal_in, "rows", axis=0, tiled=True)
    gate_proj = jnp.dot(normal_in, w_gate, preferred_element_type=jnp.float32)
    up_proj = jnp.dot(normal_in, w_up, preferred_element_type=jnp.float32)
    hidden_units = (jax.nn.gelu(gate_proj, approximate=True) * up_proj).astype(jnp.bfloat16)
    target = jnp.dot(hidden_units, w_down, preferred_element_type=jnp.float32)

    row_size = lax.axis_size("rows")
    own_tokens, features = normal_in.shape
    factor = 1.0 / math.sqrt(own_tokens * row_size)
    own_pre = jnp.dot(tok_rows, w_enc, preferred_element_type=jnp.float32) + b_enc.astype(
        jnp.float32
    )
    own_rect = jnp.maximum(own_pre, 0.0)
    own_latent = (own_rect * own_rect).astype(jnp.bfloat16)
    recon = jnp.dot(own_latent, w_dec, preferred_element_type=jnp.float32)
    own_block = (jnp.arange(row_size) == lax.axis_index("rows"))[:, None, None]
    part = recon.reshape(row_size, own_tokens, features) - jnp.where(own_block, target[None], 0.0)
    part = part.reshape(row_size * own_tokens, features).astype(jnp.bfloat16)
    mis_rows = total_over_devices(part, b_dec.reshape(1, features), z_size)

    dec_total = contract_first(own_latent, mis_rows)
    own_slope = (contract_last(mis_rows, w_dec) * 2.0 * own_rect).astype(jnp.bfloat16)
    enc_total = contract_first(tok_rows, own_slope)
    return (enc_total * factor, dec_total * factor)


def solution(mesh):
    return jax.shard_map(
        functools.partial(on_device, mesh.shape["hidden"] // 2),
        mesh=mesh,
        in_specs=(
            P("rows", None),
            P(),
            P(None, "hidden"),
            P(None, "hidden"),
            P("hidden", None),
            P(None, ("rows", "hidden")),
            P(("rows", "hidden")),
            P(("rows", "hidden"), None),
            P(),
        ),
        out_specs=(P(None, ("rows", "hidden")), P(("rows", "hidden"), None)),
        check_vma=False,
    )
```

```python
import functools
import math

import jax
import jax.numpy as jnp
from jax import lax
from jax.experimental import pallas as pl
from jax.experimental.pallas import tpu as pltpu
from jax.sharding import PartitionSpec as P

LANES = 128


def normed(resid_stream, pre_gain):
    values = resid_stream.astype(jnp.float32)
    variance = jnp.mean(values * values, axis=-1, keepdims=True)
    return (values * lax.rsqrt(variance + 1e-06) * (1.0 + pre_gain)).astype(jnp.bfloat16)


def contract_first(left, right):
    return lax.dot_general(
        left, right, (((0,), (0,)), ((), ())), preferred_element_type=jnp.float32
    )


def contract_last(left, right):
    return lax.dot_general(
        left, right, (((1,), (1,)), ((), ())), preferred_element_type=jnp.float32
    )


def by_rows(count, block, body):
    def step(i, carry):
        body(pl.multiple_of(i * block, block))
        return carry

    lax.fori_loop(0, count // block, step, 0)


def groups_of(half):
    return [(at, LANES) for at in range(0, half, LANES)]


LAGS = (0, 2, 3, 4, 5, 6, 8, 9)


def total_kernel(
    z_size, part_ref, bias_ref, out_ref,
    core_in, acc0, in1, acc1, in2, acc2, in3, send_sem, recv_sem,
):
    tokens, features = part_ref.shape
    half_f = features // 2
    groups = groups_of(half_f)
    row, hid = lax.axis_index("rows"), lax.axis_index("hidden")
    x, core = row // 2, row % 2
    z, y = hid // 2, hid % 2
    core_peer = {"rows": x * 2 + (1 - core), "hidden": hid}
    x_peer = {"rows": (1 - x) * 2 + core, "hidden": hid}
    y_peer = {"rows": row, "hidden": z * 2 + (1 - y)}
    z_peers = [
        {"rows": row, "hidden": lax.rem(z + d, z_size) * 2 + y} for d in range(1, z_size)
    ]
    stages = 2 * (3 + z_size - 1)

    barrier = pltpu.get_barrier_semaphore()
    peers = [core_peer, x_peer, y_peer] + z_peers
    for peer in peers:
        pl.semaphore_signal(barrier, inc=1, device_id=peer, device_id_type=pl.DeviceIdType.MESH)
    pl.semaphore_wait(barrier, len(peers))

    def copy(group, stage, src, dst, peer):
        at = group * stages + stage
        return pltpu.make_async_remote_copy(
            src_ref=src, dst_ref=dst, send_sem=send_sem.at[at], recv_sem=recv_sem.at[at],
            device_id=peer, device_id_type=pl.DeviceIdType.MESH,
        )

    t1, t2, t3 = tokens // 2, tokens // 4, tokens // (4 * z_size)
    started = []

    def go(copies):
        for c in copies:
            c.start()
        started.extend(copies)
        return copies

    def mine(off, width):
        return pl.ds(pl.multiple_of(core * half_f + off, LANES), width)

    def rows_at(start, size):
        return pl.ds(pl.multiple_of(start, size), size)

    def bits(g):
        return (x, y, x_peer, y_peer) if g % 2 == 0 else (y, x, y_peer, x_peer)

    base = 3 + z_size - 1
    flying = []
    for g, (off, width) in enumerate(groups):
        theirs = pl.ds(pl.multiple_of((1 - core) * half_f + off, LANES), width)
        flying.append(go([copy(g, 0, part_ref.at[:, theirs], core_in.at[:, pl.ds(off, width)], core_peer)]))

    def sum_cores(g):
        off, width = groups[g]
        b1, b2, p1, p2 = bits(g)
        cols, own = pl.ds(off, width), mine(off, width)

        def add(i):
            rows = pl.ds(i, 128)
            acc0[rows, cols] = (
                part_ref[rows, own].astype(jnp.float32) + core_in[rows, cols].astype(jnp.float32)
            ).astype(jnp.bfloat16)

        by_rows(tokens, 128, add)
        return [copy(g, 1, acc0.at[rows_at((1 - b1) * t1, t1), cols], in1.at[:, cols], p1)]

    def sum_first(g):
        off, width = groups[g]
        b1, b2, p1, p2 = bits(g)
        cols = pl.ds(off, width)

        def add(i):
            kept = pl.ds(pl.multiple_of(b1 * t1 + i, 128), 128)
            rows = pl.ds(i, 128)
            acc1[rows, cols] = (
                acc0[kept, cols].astype(jnp.float32) + in1[rows, cols].astype(jnp.float32)
            ).astype(jnp.bfloat16)

        by_rows(t1, 128, add)
        return [copy(g, 2, acc1.at[rows_at((1 - b2) * t2, t2), cols], in2.at[:, cols], p2)]

    def sum_second(g):
        off, width = groups[g]
        b1, b2, p1, p2 = bits(g)
        cols = pl.ds(off, width)

        def add(i):
            kept = pl.ds(pl.multiple_of(b2 * t2 + i, 128), 128)
            rows = pl.ds(i, 128)
            acc2[rows, cols] = (
                acc1[kept, cols].astype(jnp.float32) + in2[rows, cols].astype(jnp.float32)
            ).astype(jnp.bfloat16)

        by_rows(t2, 128, add)
        return [
            copy(g, 3 + d, acc2.at[rows_at(lax.rem(z + 1 + d, z_size) * t3, t3), cols],
                 in3.at[d, :, cols], z_peers[d])
            for d in range(z_size - 1)
        ]

    def sum_last(g):
        off, width = groups[g]
        b1, b2, p1, p2 = bits(g)
        cols, own = pl.ds(off, width), mine(off, width)
        start = b1 * t1 + b2 * t2 + z * t3
        total = acc2[rows_at(z * t3, t3), cols].astype(jnp.float32)
        for d in range(z_size - 1):
            total = total + in3[d, :, cols].astype(jnp.float32)
        out_ref[rows_at(start, t3), own] = (total + bias_ref[:, own]).astype(jnp.bfloat16)
        block = out_ref.at[rows_at(start, t3), own]
        return [copy(g, base + d, block, block, z_peers[d]) for d in range(z_size - 1)]

    def give_quarter(g):
        b1, b2, p1, p2 = bits(g)
        block = out_ref.at[rows_at(b1 * t1 + b2 * t2, t2), mine(*groups[g])]
        return [copy(g, base + z_size - 1, block, block, p2)]

    def give_half(g):
        b1, b2, p1, p2 = bits(g)
        block = out_ref.at[rows_at(b1 * t1, t1), mine(*groups[g])]
        return [copy(g, base + z_size, block, block, p1)]

    def give_core(g):
        block = out_ref.at[:, mine(*groups[g])]
        return [copy(g, base + z_size + 1, block, block, core_peer)]

    def end(g):
        return []

    work = (sum_cores, sum_first, sum_second, sum_last, give_quarter, give_half, give_core, end)
    count = len(groups)
    for step in range((count + 1) // 2 + LAGS[-1]):
        for stage in (0,) + tuple(range(len(work) - 1, 0, -1)):
            pair = step - LAGS[stage]
            for g in (2 * pair, 2 * pair + 1):
                if 0 <= g < count:
                    for c in flying[g]:
                        c.wait_recv()
                    flying[g] = go(work[stage](g))

    for c in started:
        c.wait_send()


def total_over_devices(part, bias, z_size):
    tokens, features = part.shape
    half_f = features // 2
    stages = 2 * (3 + z_size - 1) * len(groups_of(half_f))
    t1, t2, t3 = tokens // 2, tokens // 4, tokens // (4 * z_size)
    bf = jnp.bfloat16
    return pl.pallas_call(
        functools.partial(total_kernel, z_size),
        out_shape=jax.ShapeDtypeStruct((tokens, features), bf),
        in_specs=[pl.BlockSpec(memory_space=pltpu.VMEM)] * 2,
        out_specs=pl.BlockSpec(memory_space=pltpu.VMEM),
        scratch_shapes=[
            pltpu.VMEM((tokens, half_f), bf),
            pltpu.VMEM((tokens, half_f), bf),
            pltpu.VMEM((t1, half_f), bf),
            pltpu.VMEM((t1, half_f), bf),
            pltpu.VMEM((t2, half_f), bf),
            pltpu.VMEM((t2, half_f), bf),
            pltpu.VMEM((z_size - 1, t3, half_f), bf),
            pltpu.SemaphoreType.DMA((stages,)),
            pltpu.SemaphoreType.DMA((stages,)),
        ],
        compiler_params=pltpu.CompilerParams(
            collective_id=0, has_side_effects=True, vmem_limit_bytes=48 * 1024 * 1024
        ),
    )(part, bias)


def swap(values, axis, distance):
    return lax.ppermute(values, axis, [(i, i ^ distance) for i in range(lax.axis_size(axis))])


def gather_tokens(own):
    count, features = own.shape
    row, y = lax.axis_index("rows"), lax.axis_index("hidden") % 2
    pieces = 2
    size = count // (2 * pieces)
    everyone = jnp.zeros((lax.axis_size("rows") * count, features), own.dtype)

    def place(everyone, values, start):
        return lax.dynamic_update_slice_in_dim(everyone, values, start, 0)

    over_x = [
        swap(lax.dynamic_slice_in_dim(own, y * (count // 2) + i * size, size, 0), "rows", 2)
        for i in range(pieces)
    ]
    over_y = [swap(values, "hidden", 1) for values in over_x]
    on_chip = swap(own, "rows", 1)
    everyone = place(everyone, own, row * count)
    everyone = place(everyone, on_chip, (row ^ 1) * count)
    across = (row ^ 2) * count
    far = [swap(values, "rows", 1) for values in over_x + over_y]
    near_far = (row ^ 3) * count
    for i in range(pieces):
        here = y * (count // 2) + i * size
        there = (1 - y) * (count // 2) + i * size
        everyone = place(everyone, over_x[i], across + here)
        everyone = place(everyone, over_y[i], across + there)
        everyone = place(everyone, far[i], near_far + here)
        everyone = place(everyone, far[pieces + i], near_far + there)
    return everyone


def on_device(z_size, resid_stream, pre_gain, w_gate, w_up, w_down, w_enc, b_enc, w_dec, b_dec):
    normal_in = normed(resid_stream, pre_gain)
    tok_rows = gather_tokens(normal_in)
    gate_proj = jnp.dot(normal_in, w_gate, preferred_element_type=jnp.float32)
    up_proj = jnp.dot(normal_in, w_up, preferred_element_type=jnp.float32)
    hidden_units = (jax.nn.gelu(gate_proj, approximate=True) * up_proj).astype(jnp.bfloat16)
    target = jnp.dot(hidden_units, w_down, preferred_element_type=jnp.float32)

    row_size = lax.axis_size("rows")
    own_tokens, features = normal_in.shape
    factor = 1.0 / math.sqrt(own_tokens * row_size)
    own_pre = jnp.dot(tok_rows, w_enc, preferred_element_type=jnp.float32) + b_enc.astype(
        jnp.float32
    )
    own_rect = jnp.maximum(own_pre, 0.0)
    own_latent = (own_rect * own_rect).astype(jnp.bfloat16)
    recon = jnp.dot(own_latent, w_dec, preferred_element_type=jnp.float32)
    own_block = (jnp.arange(row_size) == lax.axis_index("rows"))[:, None, None]
    part = recon.reshape(row_size, own_tokens, features) - jnp.where(own_block, target[None], 0.0)
    part = part.reshape(row_size * own_tokens, features).astype(jnp.bfloat16)
    mis_rows = total_over_devices(part, b_dec.reshape(1, features), z_size)

    dec_total = contract_first(own_latent, mis_rows)
    own_slope = (contract_last(mis_rows, w_dec) * 2.0 * own_rect).astype(jnp.bfloat16)
    enc_total = contract_first(tok_rows, own_slope)
    return (enc_total * factor, dec_total * factor)


def solution(mesh):
    return jax.shard_map(
        functools.partial(on_device, mesh.shape["hidden"] // 2),
        mesh=mesh,
        in_specs=(
            P("rows", None),
            P(),
            P(None, "hidden"),
            P(None, "hidden"),
            P("hidden", None),
            P(None, ("rows", "hidden")),
            P(("rows", "hidden")),
            P(("rows", "hidden"), None),
            P(),
        ),
        out_specs=(P(None, ("rows", "hidden")), P(("rows", "hidden"), None)),
        check_vma=False,
    )
```

```python
import functools
import math

import jax
import jax.numpy as jnp
from jax import lax
from jax.experimental import pallas as pl
from jax.experimental.pallas import tpu as pltpu
from jax.sharding import PartitionSpec as P

LANES = 128


def normed(resid_stream, pre_gain):
    values = resid_stream.astype(jnp.float32)
    variance = jnp.mean(values * values, axis=-1, keepdims=True)
    return (values * lax.rsqrt(variance + 1e-06) * (1.0 + pre_gain)).astype(jnp.bfloat16)


def contract_first(left, right):
    return lax.dot_general(
        left, right, (((0,), (0,)), ((), ())), preferred_element_type=jnp.float32
    )


def contract_last(left, right):
    return lax.dot_general(
        left, right, (((1,), (1,)), ((), ())), preferred_element_type=jnp.float32
    )


def by_rows(count, block, body):
    def step(i, carry):
        body(pl.multiple_of(i * block, block))
        return carry

    lax.fori_loop(0, count // block, step, 0)


def groups_of(half):
    return [(at, LANES) for at in range(0, half, LANES)]


LAGS = (0, 2, 3, 4, 5, 6, 8, 9)


def total_kernel(
    z_size, part_ref, bias_ref, out_ref,
    core_in, acc0, in1, acc1, in2, acc2, in3, send_sem, recv_sem,
):
    tokens, features = part_ref.shape
    half_f = features // 2
    groups = groups_of(half_f)
    row, hid = lax.axis_index("rows"), lax.axis_index("hidden")
    x, core = row // 2, row % 2
    z, y = hid // 2, hid % 2
    core_peer = {"rows": x * 2 + (1 - core), "hidden": hid}
    x_peer = {"rows": (1 - x) * 2 + core, "hidden": hid}
    y_peer = {"rows": row, "hidden": z * 2 + (1 - y)}
    z_peers = [
        {"rows": row, "hidden": lax.rem(z + d, z_size) * 2 + y} for d in range(1, z_size)
    ]
    stages = 2 * (3 + z_size - 1)

    barrier = pltpu.get_barrier_semaphore()
    peers = [core_peer, x_peer, y_peer] + z_peers
    for peer in peers:
        pl.semaphore_signal(barrier, inc=1, device_id=peer, device_id_type=pl.DeviceIdType.MESH)
    pl.semaphore_wait(barrier, len(peers))

    def copy(group, stage, src, dst, peer):
        at = group * stages + stage
        return pltpu.make_async_remote_copy(
            src_ref=src, dst_ref=dst, send_sem=send_sem.at[at], recv_sem=recv_sem.at[at],
            device_id=peer, device_id_type=pl.DeviceIdType.MESH,
        )

    t1, t2, t3 = tokens // 2, tokens // 4, tokens // (4 * z_size)
    started = []

    def go(copies):
        for c in copies:
            c.start()
        started.extend(copies)
        return copies

    def mine(off, width):
        return pl.ds(pl.multiple_of(core * half_f + off, LANES), width)

    def rows_at(start, size):
        return pl.ds(pl.multiple_of(start, size), size)

    def bits(g):
        return (x, y, x_peer, y_peer) if g % 2 == 0 else (y, x, y_peer, x_peer)

    base = 3 + z_size - 1
    flying = []
    for g, (off, width) in enumerate(groups):
        theirs = pl.ds(pl.multiple_of((1 - core) * half_f + off, LANES), width)
        flying.append(go([copy(g, 0, part_ref.at[:, theirs], core_in.at[:, pl.ds(off, width)], core_peer)]))

    def sum_cores(g):
        off, width = groups[g]
        b1, b2, p1, p2 = bits(g)
        cols, own = pl.ds(off, width), mine(off, width)

        def add(i):
            rows = pl.ds(i, 128)
            acc0[rows, cols] = (
                part_ref[rows, own].astype(jnp.float32) + core_in[rows, cols].astype(jnp.float32)
            ).astype(jnp.bfloat16)

        by_rows(tokens, 128, add)
        return [copy(g, 1, acc0.at[rows_at((1 - b1) * t1, t1), cols], in1.at[:, cols], p1)]

    def sum_first(g):
        off, width = groups[g]
        b1, b2, p1, p2 = bits(g)
        cols = pl.ds(off, width)

        def add(i):
            kept = pl.ds(pl.multiple_of(b1 * t1 + i, 128), 128)
            rows = pl.ds(i, 128)
            acc1[rows, cols] = (
                acc0[kept, cols].astype(jnp.float32) + in1[rows, cols].astype(jnp.float32)
            ).astype(jnp.bfloat16)

        by_rows(t1, 128, add)
        return [copy(g, 2, acc1.at[rows_at((1 - b2) * t2, t2), cols], in2.at[:, cols], p2)]

    def sum_second(g):
        off, width = groups[g]
        b1, b2, p1, p2 = bits(g)
        cols = pl.ds(off, width)

        def add(i):
            kept = pl.ds(pl.multiple_of(b2 * t2 + i, 128), 128)
            rows = pl.ds(i, 128)
            acc2[rows, cols] = (
                acc1[kept, cols].astype(jnp.float32) + in2[rows, cols].astype(jnp.float32)
            ).astype(jnp.bfloat16)

        by_rows(t2, 128, add)
        return [
            copy(g, 3 + d, acc2.at[rows_at(lax.rem(z + 1 + d, z_size) * t3, t3), cols],
                 in3.at[d, :, cols], z_peers[d])
            for d in range(z_size - 1)
        ]

    def sum_last(g):
        off, width = groups[g]
        b1, b2, p1, p2 = bits(g)
        cols, own = pl.ds(off, width), mine(off, width)
        start = b1 * t1 + b2 * t2 + z * t3
        total = acc2[rows_at(z * t3, t3), cols].astype(jnp.float32)
        for d in range(z_size - 1):
            total = total + in3[d, :, cols].astype(jnp.float32)
        out_ref[rows_at(start, t3), own] = (total + bias_ref[:, own]).astype(jnp.bfloat16)
        block = out_ref.at[rows_at(start, t3), own]
        return [copy(g, base + d, block, block, z_peers[d]) for d in range(z_size - 1)]

    def give_quarter(g):
        b1, b2, p1, p2 = bits(g)
        block = out_ref.at[rows_at(b1 * t1 + b2 * t2, t2), mine(*groups[g])]
        return [copy(g, base + z_size - 1, block, block, p2)]

    def give_half(g):
        b1, b2, p1, p2 = bits(g)
        block = out_ref.at[rows_at(b1 * t1, t1), mine(*groups[g])]
        return [copy(g, base + z_size, block, block, p1)]

    def give_core(g):
        block = out_ref.at[:, mine(*groups[g])]
        return [copy(g, base + z_size + 1, block, block, core_peer)]

    def end(g):
        return []

    work = (sum_cores, sum_first, sum_second, sum_last, give_quarter, give_half, give_core, end)
    count = len(groups)
    for step in range((count + 1) // 2 + LAGS[-1]):
        for stage in (0,) + tuple(range(len(work) - 1, 0, -1)):
            pair = step - LAGS[stage]
            for g in (2 * pair, 2 * pair + 1):
                if 0 <= g < count:
                    for c in flying[g]:
                        c.wait_recv()
                    flying[g] = go(work[stage](g))

    for c in started:
        c.wait_send()


def total_over_devices(part, bias, z_size):
    tokens, features = part.shape
    half_f = features // 2
    stages = 2 * (3 + z_size - 1) * len(groups_of(half_f))
    t1, t2, t3 = tokens // 2, tokens // 4, tokens // (4 * z_size)
    bf = jnp.bfloat16
    return pl.pallas_call(
        functools.partial(total_kernel, z_size),
        out_shape=jax.ShapeDtypeStruct((tokens, features), bf),
        in_specs=[pl.BlockSpec(memory_space=pltpu.VMEM)] * 2,
        out_specs=pl.BlockSpec(memory_space=pltpu.VMEM),
        scratch_shapes=[
            pltpu.VMEM((tokens, half_f), bf),
            pltpu.VMEM((tokens, half_f), bf),
            pltpu.VMEM((t1, half_f), bf),
            pltpu.VMEM((t1, half_f), bf),
            pltpu.VMEM((t2, half_f), bf),
            pltpu.VMEM((t2, half_f), bf),
            pltpu.VMEM((z_size - 1, t3, half_f), bf),
            pltpu.SemaphoreType.DMA((stages,)),
            pltpu.SemaphoreType.DMA((stages,)),
        ],
        compiler_params=pltpu.CompilerParams(
            collective_id=0, has_side_effects=True, vmem_limit_bytes=48 * 1024 * 1024
        ),
    )(part, bias)


PIECES = 4


def widest(size, options):
    return next(w for w in options if size % w == 0)


def mlp_kernel(
    own_ref, gate_ref, up_ref, down_ref, tok_ref, target_ref,
    hidden, gates, ups, downs, load_sem, own_sem, send_sem, recv_sem,
):
    count, features = own_ref.shape
    row, hid = lax.axis_index("rows"), lax.axis_index("hidden")
    x, core, z, y = row // 2, row % 2, hid // 2, hid % 2
    across = (1 - x) * 2 + core
    core_peer = {"rows": x * 2 + (1 - core), "hidden": hid}
    x_peer = {"rows": across, "hidden": hid}
    y_peer = {"rows": row, "hidden": z * 2 + (1 - y)}
    barrier = pltpu.get_barrier_semaphore()
    for peer in (core_peer, x_peer, y_peer):
        pl.semaphore_signal(barrier, inc=1, device_id=peer, device_id_type=pl.DeviceIdType.MESH)
    pl.semaphore_wait(barrier, 3)

    half = count // 2
    size = half // PIECES

    def copy(at, src, dst, peer):
        return pltpu.make_async_remote_copy(
            src_ref=src, dst_ref=dst, send_sem=send_sem.at[at], recv_sem=recv_sem.at[at],
            device_id=peer, device_id_type=pl.DeviceIdType.MESH,
        )

    def tok(start, rows):
        return tok_ref.at[pl.ds(pl.multiple_of(start, rows), rows), :]

    mine = tok(row * count, count)
    place = pltpu.make_async_copy(own_ref, mine, own_sem)
    to_core = copy(0, own_ref, mine, core_peer)
    over_x, over_y, core_x, core_y = [], [], [], []
    for i in range(PIECES):
        here = y * half + i * size
        there = (1 - y) * half + i * size
        piece = own_ref.at[pl.ds(pl.multiple_of(here, size), size), :]
        over_x.append(copy(1 + i, piece, tok(row * count + here, size), x_peer))
        got = tok(across * count + here, size)
        far = tok(across * count + there, size)
        over_y.append(copy(1 + PIECES + i, got, got, y_peer))
        core_x.append(copy(1 + 2 * PIECES + i, got, got, core_peer))
        core_y.append(copy(1 + 3 * PIECES + i, far, far, core_peer))

    for c in over_x:
        c.start()
    to_core.start()
    place.start()

    def took_x(i):
        over_x[i].wait_recv()
        over_y[i].start()
        core_x[i].start()

    def took_y(i):
        over_y[i].wait_recv()
        core_y[i].start()

    width, down_width = gates.shape[2], downs.shape[2]
    steps, down_steps = gate_ref.shape[1] // width, features // down_width

    def tile(i, width, count):
        return pl.ds(0 if count == 1 else pl.multiple_of(i * width, width), width)

    def loads(i):
        slot = lax.rem(i, 2)
        cols = tile(i, width, steps)
        return (
            pltpu.make_async_copy(gate_ref.at[:, cols], gates.at[slot], load_sem.at[slot]),
            pltpu.make_async_copy(up_ref.at[:, cols], ups.at[slot], load_sem.at[2 + slot]),
        )

    def down_loads(i):
        slot = lax.rem(i, 2)
        cols = pl.ds(pl.multiple_of(i * down_width, down_width), down_width)
        return (pltpu.make_async_copy(down_ref.at[:, cols], downs.at[slot], load_sem.at[4 + slot]),)

    def start(copies):
        for c in copies:
            c.start()

    def gate_step(i, carry):
        @pl.when(i + 1 < steps)
        def _():
            start(loads(i + 1))

        for c in loads(i):
            c.wait()
        slot = lax.rem(i, 2)
        gate = jnp.dot(own_ref[...], gates[slot], preferred_element_type=jnp.float32)
        up = jnp.dot(own_ref[...], ups[slot], preferred_element_type=jnp.float32)
        hidden[:, tile(i, width, steps)] = (
            jax.nn.gelu(gate, approximate=True) * up
        ).astype(jnp.bfloat16)
        return carry

    def down_step(i, carry):
        @pl.when(i + 1 < down_steps)
        def _():
            start(down_loads(i + 1))

        for c in down_loads(i):
            c.wait()
        target_ref[:, pl.ds(pl.multiple_of(i * down_width, down_width), down_width)] = jnp.dot(
            hidden[...], downs[lax.rem(i, 2)], preferred_element_type=jnp.float32
        )
        return carry

    start(loads(0))
    start(down_loads(0))
    done = 0
    for i in range(PIECES):
        until = min(steps, 2 * (i + 1))
        lax.fori_loop(done, until, gate_step, 0)
        done = until
        took_x(i)
        if i:
            took_y(i - 1)
    lax.fori_loop(done, steps, gate_step, 0)
    middle = (down_steps * 2) // 3
    lax.fori_loop(0, middle, down_step, 0)
    took_y(PIECES - 1)
    lax.fori_loop(middle, down_steps, down_step, 0)

    place.wait()
    to_core.wait_recv()
    for c in core_x + core_y:
        c.wait_recv()
    for c in [to_core] + over_x + over_y + core_x + core_y:
        c.wait_send()


def gather_and_mlp(own, w_gate, w_up, w_down):
    count, features = own.shape
    units = w_gate.shape[1]
    width = widest(units, (256, 128, units))
    down_width = widest(features, (512, 256, 128))
    bf = jnp.bfloat16
    copies = 1 + 4 * PIECES
    vmem, anywhere = pl.BlockSpec(memory_space=pltpu.VMEM), pl.BlockSpec(memory_space=pl.ANY)
    return pl.pallas_call(
        mlp_kernel,
        out_shape=(
            jax.ShapeDtypeStruct((lax.axis_size("rows") * count, features), bf),
            jax.ShapeDtypeStruct((count, features), jnp.float32),
        ),
        in_specs=[vmem, anywhere, anywhere, anywhere],
        out_specs=(vmem, vmem),
        scratch_shapes=[
            pltpu.VMEM((count, units), bf),
            pltpu.VMEM((2, features, width), bf),
            pltpu.VMEM((2, features, width), bf),
            pltpu.VMEM((2, units, down_width), bf),
            pltpu.SemaphoreType.DMA((6,)),
            pltpu.SemaphoreType.DMA,
            pltpu.SemaphoreType.DMA((copies,)),
            pltpu.SemaphoreType.DMA((copies,)),
        ],
        compiler_params=pltpu.CompilerParams(
            collective_id=1, has_side_effects=True, vmem_limit_bytes=48 * 1024 * 1024
        ),
    )(own, w_gate, w_up, w_down)


def on_device(z_size, resid_stream, pre_gain, w_gate, w_up, w_down, w_enc, b_enc, w_dec, b_dec):
    normal_in = normed(resid_stream, pre_gain)
    tok_rows, target = gather_and_mlp(normal_in, w_gate, w_up, w_down)
    row_size = lax.axis_size("rows")
    own_tokens, features = normal_in.shape
    factor = 1.0 / math.sqrt(own_tokens * row_size)
    own_pre = jnp.dot(tok_rows, w_enc, preferred_element_type=jnp.float32) + b_enc.astype(
        jnp.float32
    )
    own_rect = jnp.maximum(own_pre, 0.0)
    own_latent = (own_rect * own_rect).astype(jnp.bfloat16)
    recon = jnp.dot(own_latent, w_dec, preferred_element_type=jnp.float32)
    own_block = (jnp.arange(row_size) == lax.axis_index("rows"))[:, None, None]
    part = recon.reshape(row_size, own_tokens, features) - jnp.where(own_block, target[None], 0.0)
    part = part.reshape(row_size * own_tokens, features).astype(jnp.bfloat16)
    mis_rows = total_over_devices(part, b_dec.reshape(1, features), z_size)

    dec_total = contract_first(own_latent, mis_rows)
    own_slope = (contract_last(mis_rows, w_dec) * 2.0 * own_rect).astype(jnp.bfloat16)
    enc_total = contract_first(tok_rows, own_slope)
    return (enc_total * factor, dec_total * factor)


def solution(mesh):
    return jax.shard_map(
        functools.partial(on_device, mesh.shape["hidden"] // 2),
        mesh=mesh,
        in_specs=(
            P("rows", None),
            P(),
            P(None, "hidden"),
            P(None, "hidden"),
            P("hidden", None),
            P(None, ("rows", "hidden")),
            P(("rows", "hidden")),
            P(("rows", "hidden"), None),
            P(),
        ),
        out_specs=(P(None, ("rows", "hidden")), P(("rows", "hidden"), None)),
        check_vma=False,
    )
```

```python
import functools
import math

import jax
import jax.numpy as jnp
from jax import lax
from jax.experimental import pallas as pl
from jax.experimental.pallas import tpu as pltpu
from jax.sharding import PartitionSpec as P

LANES = 128


def normed(resid_stream, pre_gain):
    values = resid_stream.astype(jnp.float32)
    variance = jnp.mean(values * values, axis=-1, keepdims=True)
    return (values * lax.rsqrt(variance + 1e-06) * (1.0 + pre_gain)).astype(jnp.bfloat16)


def contract_first(left, right):
    return lax.dot_general(
        left, right, (((0,), (0,)), ((), ())), preferred_element_type=jnp.float32
    )


def contract_last(left, right):
    return lax.dot_general(
        left, right, (((1,), (1,)), ((), ())), preferred_element_type=jnp.float32
    )


def by_rows(count, block, body):
    def step(i, carry):
        body(pl.multiple_of(i * block, block))
        return carry

    lax.fori_loop(0, count // block, step, 0)


def groups_of(half):
    return [(at, LANES) for at in range(0, half, LANES)]


LAGS = (0, 2, 3, 4, 5, 6, 8, 9)


def total_kernel(
    z_size, factor, latent_ref, turned_ref, rect_ref, dec_ref, target_ref, bias_ref,
    dec_grad_ref, slope_ref,
    part_ref, out_ref, back_prop, core_in, acc0, in1, acc1, in2, acc2, in3, send_sem, recv_sem,
):
    tokens, features = out_ref.shape
    half_f = features // 2
    groups = groups_of(half_f)
    row, hid = lax.axis_index("rows"), lax.axis_index("hidden")
    x, core = row // 2, row % 2
    z, y = hid // 2, hid % 2
    core_peer = {"rows": x * 2 + (1 - core), "hidden": hid}
    x_peer = {"rows": (1 - x) * 2 + core, "hidden": hid}
    y_peer = {"rows": row, "hidden": z * 2 + (1 - y)}
    z_peers = [
        {"rows": row, "hidden": lax.rem(z + d, z_size) * 2 + y} for d in range(1, z_size)
    ]
    stages = 2 * (3 + z_size - 1)

    barrier = pltpu.get_barrier_semaphore()
    peers = [core_peer, x_peer, y_peer] + z_peers
    for peer in peers:
        pl.semaphore_signal(barrier, inc=1, device_id=peer, device_id_type=pl.DeviceIdType.MESH)
    pl.semaphore_wait(barrier, len(peers))

    def copy(group, stage, src, dst, peer):
        at = group * stages + stage
        return pltpu.make_async_remote_copy(
            src_ref=src, dst_ref=dst, send_sem=send_sem.at[at], recv_sem=recv_sem.at[at],
            device_id=peer, device_id_type=pl.DeviceIdType.MESH,
        )

    t1, t2, t3 = tokens // 2, tokens // 4, tokens // (4 * z_size)
    started = []

    def go(copies):
        for c in copies:
            c.start()
        started.extend(copies)
        return copies

    def mine(off, width):
        return pl.ds(pl.multiple_of(core * half_f + off, LANES), width)

    def rows_at(start, size):
        return pl.ds(pl.multiple_of(start, size), size)

    def bits(g):
        return (x, y, x_peer, y_peer) if g % 2 == 0 else (y, x, y_peer, x_peer)

    base = 3 + z_size - 1
    flying = [[] for _ in groups]
    own_tokens = target_ref.shape[0]
    count = len(groups)

    def pair_cols(pair, side):
        width = sum(w for _, w in groups[2 * pair : 2 * pair + 2])
        return pl.ds(pl.multiple_of(side * half_f + 2 * pair * LANES, LANES), width)

    def term(i, cols):
        product = jnp.dot(
            latent_ref[pl.ds(i, own_tokens), :], dec_ref[:, cols], preferred_element_type=jnp.float32
        )
        return product - jnp.where(i == row * own_tokens, target_ref[:, cols], 0.0)

    def make(pair):
        if 2 * pair >= count:
            return
        cols = pair_cols(pair, 1 - core)

        def fill(i):
            part_ref[pl.ds(i, own_tokens), cols] = term(i, cols).astype(jnp.bfloat16)

        by_rows(tokens, own_tokens, fill)
        for g in range(2 * pair, min(2 * pair + 2, count)):
            off, width = groups[g]
            theirs = pl.ds(pl.multiple_of((1 - core) * half_f + off, LANES), width)
            flying[g] = go([
                copy(g, 0, part_ref.at[:, theirs], core_in.at[:, pl.ds(off, width)], core_peer)
            ])

    def use(pair, side):
        cols = pair_cols(pair, side)
        dec_grad_ref[:, cols] = (
            jnp.dot(turned_ref[...], out_ref[:, cols], preferred_element_type=jnp.float32) * factor
        )

        def add(i):
            rows = pl.ds(i, own_tokens)
            back_prop[rows, :] += contract_last(out_ref[rows, cols], dec_ref[:, cols])

        by_rows(tokens, own_tokens, add)

    make(0)
    back_prop[...] = jnp.zeros_like(back_prop)
    make(1)

    def sum_cores(g):
        off, width = groups[g]
        b1, b2, p1, p2 = bits(g)
        cols, own = pl.ds(off, width), mine(off, width)

        def add(i):
            rows = pl.ds(i, own_tokens)
            acc0[rows, cols] = (term(i, own) + core_in[rows, cols].astype(jnp.float32)).astype(
                jnp.bfloat16
            )

        by_rows(tokens, own_tokens, add)
        return [copy(g, 1, acc0.at[rows_at((1 - b1) * t1, t1), cols], in1.at[:, cols], p1)]

    def sum_first(g):
        off, width = groups[g]
        b1, b2, p1, p2 = bits(g)
        cols = pl.ds(off, width)

        def add(i):
            kept = pl.ds(pl.multiple_of(b1 * t1 + i, 128), 128)
            rows = pl.ds(i, 128)
            acc1[rows, cols] = (
                acc0[kept, cols].astype(jnp.float32) + in1[rows, cols].astype(jnp.float32)
            ).astype(jnp.bfloat16)

        by_rows(t1, 128, add)
        return [copy(g, 2, acc1.at[rows_at((1 - b2) * t2, t2), cols], in2.at[:, cols], p2)]

    def sum_second(g):
        off, width = groups[g]
        b1, b2, p1, p2 = bits(g)
        cols = pl.ds(off, width)

        def add(i):
            kept = pl.ds(pl.multiple_of(b2 * t2 + i, 128), 128)
            rows = pl.ds(i, 128)
            acc2[rows, cols] = (
                acc1[kept, cols].astype(jnp.float32) + in2[rows, cols].astype(jnp.float32)
            ).astype(jnp.bfloat16)

        by_rows(t2, 128, add)
        return [
            copy(g, 3 + d, acc2.at[rows_at(lax.rem(z + 1 + d, z_size) * t3, t3), cols],
                 in3.at[d, :, cols], z_peers[d])
            for d in range(z_size - 1)
        ]

    def sum_last(g):
        off, width = groups[g]
        b1, b2, p1, p2 = bits(g)
        cols, own = pl.ds(off, width), mine(off, width)
        start = b1 * t1 + b2 * t2 + z * t3
        total = acc2[rows_at(z * t3, t3), cols].astype(jnp.float32)
        for d in range(z_size - 1):
            total = total + in3[d, :, cols].astype(jnp.float32)
        out_ref[rows_at(start, t3), own] = (total + bias_ref[:, own]).astype(jnp.bfloat16)
        block = out_ref.at[rows_at(start, t3), own]
        return [copy(g, base + d, block, block, z_peers[d]) for d in range(z_size - 1)]

    def give_quarter(g):
        b1, b2, p1, p2 = bits(g)
        block = out_ref.at[rows_at(b1 * t1 + b2 * t2, t2), mine(*groups[g])]
        return [copy(g, base + z_size - 1, block, block, p2)]

    def give_half(g):
        b1, b2, p1, p2 = bits(g)
        block = out_ref.at[rows_at(b1 * t1, t1), mine(*groups[g])]
        return [copy(g, base + z_size, block, block, p1)]

    def give_core(g):
        block = out_ref.at[:, mine(*groups[g])]
        return [copy(g, base + z_size + 1, block, block, core_peer)]

    def end(g):
        return []

    work = (sum_cores, sum_first, sum_second, sum_last, give_quarter, give_half, give_core, end)
    pairs = (count + 1) // 2
    for step in range(pairs + LAGS[-1]):
        for stage in (0,) + tuple(range(len(work) - 1, 0, -1)):
            pair = step - LAGS[stage]
            for g in (2 * pair, 2 * pair + 1):
                if 0 <= g < count:
                    for c in flying[g]:
                        c.wait_recv()
                    flying[g] = go(work[stage](g))
        make(step + 2)
        for stage, side in ((6, core), (7, 1 - core)):
            if 0 <= step - LAGS[stage] < pairs:
                use(step - LAGS[stage], side)

    def slopes(i):
        rows = pl.ds(i, own_tokens)
        slope_ref[rows, :] = (back_prop[rows, :] * 2.0 * rect_ref[rows, :]).astype(jnp.bfloat16)

    by_rows(tokens, own_tokens, slopes)
    for c in started:
        c.wait_send()


def total_and_grads(latent, rect, w_dec, target, bias, z_size, factor):
    tokens, own_latents = latent.shape
    features = w_dec.shape[1]
    half_f = features // 2
    stages = 2 * (3 + z_size - 1) * len(groups_of(half_f))
    t1, t2, t3 = tokens // 2, tokens // 4, tokens // (4 * z_size)
    bf = jnp.bfloat16
    return pl.pallas_call(
        functools.partial(total_kernel, z_size, factor),
        out_shape=(
            jax.ShapeDtypeStruct((own_latents, features), jnp.float32),
            jax.ShapeDtypeStruct((tokens, own_latents), bf),
        ),
        in_specs=[pl.BlockSpec(memory_space=pltpu.VMEM)] * 6,
        out_specs=(pl.BlockSpec(memory_space=pltpu.VMEM),) * 2,
        scratch_shapes=[
            pltpu.VMEM((tokens, features), bf),
            pltpu.VMEM((tokens, features), bf),
            pltpu.VMEM((tokens, own_latents), jnp.float32),
            pltpu.VMEM((tokens, half_f), bf),
            pltpu.VMEM((tokens, half_f), bf),
            pltpu.VMEM((t1, half_f), bf),
            pltpu.VMEM((t1, half_f), bf),
            pltpu.VMEM((t2, half_f), bf),
            pltpu.VMEM((t2, half_f), bf),
            pltpu.VMEM((z_size - 1, t3, half_f), bf),
            pltpu.SemaphoreType.DMA((stages,)),
            pltpu.SemaphoreType.DMA((stages,)),
        ],
        compiler_params=pltpu.CompilerParams(
            collective_id=0, has_side_effects=True, vmem_limit_bytes=56 * 1024 * 1024
        ),
    )(latent, latent.T, rect, w_dec, target, bias)


PIECES = 4


def widest(size, options):
    return next(w for w in options if size % w == 0)


def mlp_kernel(
    own_ref, gate_ref, up_ref, down_ref, tok_ref, target_ref,
    hidden, gates, ups, downs, load_sem, own_sem, send_sem, recv_sem,
):
    count, features = own_ref.shape
    row, hid = lax.axis_index("rows"), lax.axis_index("hidden")
    x, core, z, y = row // 2, row % 2, hid // 2, hid % 2
    across = (1 - x) * 2 + core
    core_peer = {"rows": x * 2 + (1 - core), "hidden": hid}
    x_peer = {"rows": across, "hidden": hid}
    y_peer = {"rows": row, "hidden": z * 2 + (1 - y)}
    barrier = pltpu.get_barrier_semaphore()
    for peer in (core_peer, x_peer, y_peer):
        pl.semaphore_signal(barrier, inc=1, device_id=peer, device_id_type=pl.DeviceIdType.MESH)
    pl.semaphore_wait(barrier, 3)

    half = count // 2
    size = half // PIECES

    def copy(at, src, dst, peer):
        return pltpu.make_async_remote_copy(
            src_ref=src, dst_ref=dst, send_sem=send_sem.at[at], recv_sem=recv_sem.at[at],
            device_id=peer, device_id_type=pl.DeviceIdType.MESH,
        )

    def tok(start, rows):
        return tok_ref.at[pl.ds(pl.multiple_of(start, rows), rows), :]

    mine = tok(row * count, count)
    place = pltpu.make_async_copy(own_ref, mine, own_sem)
    to_core = copy(0, own_ref, mine, core_peer)
    over_x, over_y, core_x, core_y = [], [], [], []
    for i in range(PIECES):
        here = y * half + i * size
        there = (1 - y) * half + i * size
        piece = own_ref.at[pl.ds(pl.multiple_of(here, size), size), :]
        over_x.append(copy(1 + i, piece, tok(row * count + here, size), x_peer))
        got = tok(across * count + here, size)
        far = tok(across * count + there, size)
        over_y.append(copy(1 + PIECES + i, got, got, y_peer))
        core_x.append(copy(1 + 2 * PIECES + i, got, got, core_peer))
        core_y.append(copy(1 + 3 * PIECES + i, far, far, core_peer))

    for c in over_x:
        c.start()
    to_core.start()
    place.start()

    def took_x(i):
        over_x[i].wait_recv()
        over_y[i].start()
        core_x[i].start()

    def took_y(i):
        over_y[i].wait_recv()
        core_y[i].start()

    width, down_width = gates.shape[2], downs.shape[2]
    steps, down_steps = gate_ref.shape[1] // width, features // down_width

    def tile(i, width, count):
        return pl.ds(0 if count == 1 else pl.multiple_of(i * width, width), width)

    def loads(i):
        slot = lax.rem(i, 2)
        cols = tile(i, width, steps)
        return (
            pltpu.make_async_copy(gate_ref.at[:, cols], gates.at[slot], load_sem.at[slot]),
            pltpu.make_async_copy(up_ref.at[:, cols], ups.at[slot], load_sem.at[2 + slot]),
        )

    def down_loads(i):
        slot = lax.rem(i, 2)
        cols = pl.ds(pl.multiple_of(i * down_width, down_width), down_width)
        return (pltpu.make_async_copy(down_ref.at[:, cols], downs.at[slot], load_sem.at[4 + slot]),)

    def start(copies):
        for c in copies:
            c.start()

    def gate_step(i, carry):
        @pl.when(i + 1 < steps)
        def _():
            start(loads(i + 1))

        for c in loads(i):
            c.wait()
        slot = lax.rem(i, 2)
        gate = jnp.dot(own_ref[...], gates[slot], preferred_element_type=jnp.float32)
        up = jnp.dot(own_ref[...], ups[slot], preferred_element_type=jnp.float32)
        hidden[:, tile(i, width, steps)] = (
            jax.nn.gelu(gate, approximate=True) * up
        ).astype(jnp.bfloat16)
        return carry

    def down_step(i, carry):
        @pl.when(i + 1 < down_steps)
        def _():
            start(down_loads(i + 1))

        for c in down_loads(i):
            c.wait()
        target_ref[:, pl.ds(pl.multiple_of(i * down_width, down_width), down_width)] = jnp.dot(
            hidden[...], downs[lax.rem(i, 2)], preferred_element_type=jnp.float32
        )
        return carry

    start(loads(0))
    start(down_loads(0))
    done = 0
    for i in range(PIECES):
        until = min(steps, 2 * (i + 1))
        lax.fori_loop(done, until, gate_step, 0)
        done = until
        took_x(i)
        if i:
            took_y(i - 1)
    lax.fori_loop(done, steps, gate_step, 0)
    middle = (down_steps * 2) // 3
    lax.fori_loop(0, middle, down_step, 0)
    took_y(PIECES - 1)
    lax.fori_loop(middle, down_steps, down_step, 0)

    place.wait()
    to_core.wait_recv()
    for c in core_x + core_y:
        c.wait_recv()
    for c in [to_core] + over_x + over_y + core_x + core_y:
        c.wait_send()


def gather_and_mlp(own, w_gate, w_up, w_down):
    count, features = own.shape
    units = w_gate.shape[1]
    width = widest(units, (256, 128, units))
    down_width = widest(features, (512, 256, 128))
    bf = jnp.bfloat16
    copies = 1 + 4 * PIECES
    vmem, anywhere = pl.BlockSpec(memory_space=pltpu.VMEM), pl.BlockSpec(memory_space=pl.ANY)
    return pl.pallas_call(
        mlp_kernel,
        out_shape=(
            jax.ShapeDtypeStruct((lax.axis_size("rows") * count, features), bf),
            jax.ShapeDtypeStruct((count, features), jnp.float32),
        ),
        in_specs=[vmem, anywhere, anywhere, anywhere],
        out_specs=(vmem, vmem),
        scratch_shapes=[
            pltpu.VMEM((count, units), bf),
            pltpu.VMEM((2, features, width), bf),
            pltpu.VMEM((2, features, width), bf),
            pltpu.VMEM((2, units, down_width), bf),
            pltpu.SemaphoreType.DMA((6,)),
            pltpu.SemaphoreType.DMA,
            pltpu.SemaphoreType.DMA((copies,)),
            pltpu.SemaphoreType.DMA((copies,)),
        ],
        compiler_params=pltpu.CompilerParams(
            collective_id=1, has_side_effects=True, vmem_limit_bytes=48 * 1024 * 1024
        ),
    )(own, w_gate, w_up, w_down)


def on_device(z_size, resid_stream, pre_gain, w_gate, w_up, w_down, w_enc, b_enc, w_dec, b_dec):
    normal_in = normed(resid_stream, pre_gain)
    tok_rows, target = gather_and_mlp(normal_in, w_gate, w_up, w_down)
    row_size = lax.axis_size("rows")
    own_tokens, features = normal_in.shape
    factor = 1.0 / math.sqrt(own_tokens * row_size)
    own_pre = jnp.dot(tok_rows, w_enc, preferred_element_type=jnp.float32) + b_enc.astype(
        jnp.float32
    )
    own_rect = jnp.maximum(own_pre, 0.0)
    own_latent = (own_rect * own_rect).astype(jnp.bfloat16)
    dec_grad, own_slope = total_and_grads(
        own_latent, own_rect, w_dec, target, b_dec.reshape(1, features), z_size, factor
    )
    return (contract_first(tok_rows, own_slope) * factor, dec_grad)


def solution(mesh):
    return jax.shard_map(
        functools.partial(on_device, mesh.shape["hidden"] // 2),
        mesh=mesh,
        in_specs=(
            P("rows", None),
            P(),
            P(None, "hidden"),
            P(None, "hidden"),
            P("hidden", None),
            P(None, ("rows", "hidden")),
            P(("rows", "hidden")),
            P(("rows", "hidden"), None),
            P(),
        ),
        out_specs=(P(None, ("rows", "hidden")), P(("rows", "hidden"), None)),
        check_vma=False,
    )
```

```python
import functools
import math

import jax
import jax.numpy as jnp
from jax import lax
from jax.experimental import pallas as pl
from jax.experimental.pallas import tpu as pltpu
from jax.sharding import PartitionSpec as P

LANES = 128


def normed(resid_stream, pre_gain):
    values = resid_stream.astype(jnp.float32)
    variance = jnp.mean(values * values, axis=-1, keepdims=True)
    return (values * lax.rsqrt(variance + 1e-06) * (1.0 + pre_gain)).astype(jnp.bfloat16)


def contract_first(left, right):
    return lax.dot_general(
        left, right, (((0,), (0,)), ((), ())), preferred_element_type=jnp.float32
    )


def contract_last(left, right):
    return lax.dot_general(
        left, right, (((1,), (1,)), ((), ())), preferred_element_type=jnp.float32
    )


def by_rows(count, block, body):
    def step(i, carry):
        body(pl.multiple_of(i * block, block))
        return carry

    lax.fori_loop(0, count // block, step, 0)


def groups_of(half):
    return [(at, LANES) for at in range(0, half, LANES)]


LAGS = (0, 2, 4, 6, 8, 10, 12, 13)


def total_kernel(
    z_size, factor, latent_ref, turned_ref, rect_ref, dec_ref, target_ref, bias_ref,
    dec_grad_ref, slope_ref,
    part_ref, out_ref, back_prop, core_in, acc0, in1, acc1, in2, acc2, in3, send_sem, recv_sem,
):
    tokens, features = out_ref.shape
    half_f = features // 2
    groups = groups_of(half_f)
    row, hid = lax.axis_index("rows"), lax.axis_index("hidden")
    x, core = row // 2, row % 2
    z, y = hid // 2, hid % 2
    core_peer = {"rows": x * 2 + (1 - core), "hidden": hid}
    x_peer = {"rows": (1 - x) * 2 + core, "hidden": hid}
    y_peer = {"rows": row, "hidden": z * 2 + (1 - y)}
    z_peers = [
        {"rows": row, "hidden": lax.rem(z + d, z_size) * 2 + y} for d in range(1, z_size)
    ]
    stages = 2 * (3 + z_size - 1)

    barrier = pltpu.get_barrier_semaphore()
    peers = [core_peer, x_peer, y_peer] + z_peers
    for peer in peers:
        pl.semaphore_signal(barrier, inc=1, device_id=peer, device_id_type=pl.DeviceIdType.MESH)
    pl.semaphore_wait(barrier, len(peers))

    def copy(group, stage, src, dst, peer):
        at = group * stages + stage
        return pltpu.make_async_remote_copy(
            src_ref=src, dst_ref=dst, send_sem=send_sem.at[at], recv_sem=recv_sem.at[at],
            device_id=peer, device_id_type=pl.DeviceIdType.MESH,
        )

    t1, t2, t3 = tokens // 2, tokens // 4, tokens // (4 * z_size)
    started = []

    def go(copies):
        for c in copies:
            c.start()
        started.extend(copies)
        return copies

    def mine(off, width):
        return pl.ds(pl.multiple_of(core * half_f + off, LANES), width)

    def rows_at(start, size):
        return pl.ds(pl.multiple_of(start, size), size)

    def bits(g):
        return (x, y, x_peer, y_peer) if g % 2 == 0 else (y, x, y_peer, x_peer)

    base = 3 + z_size - 1
    flying = [[] for _ in groups]
    own_tokens = target_ref.shape[0]
    count = len(groups)

    def pair_cols(pair, side):
        width = sum(w for _, w in groups[2 * pair : 2 * pair + 2])
        return pl.ds(pl.multiple_of(side * half_f + 2 * pair * LANES, LANES), width)

    def term(i, cols):
        product = jnp.dot(
            latent_ref[pl.ds(i, own_tokens), :], dec_ref[:, cols], preferred_element_type=jnp.float32
        )
        return product - jnp.where(i == row * own_tokens, target_ref[:, cols], 0.0)

    def make(pair):
        if 2 * pair >= count:
            return
        cols = pair_cols(pair, 1 - core)

        def fill(i):
            part_ref[pl.ds(i, own_tokens), cols] = term(i, cols).astype(jnp.bfloat16)

        by_rows(tokens, own_tokens, fill)
        for g in range(2 * pair, min(2 * pair + 2, count)):
            off, width = groups[g]
            theirs = pl.ds(pl.multiple_of((1 - core) * half_f + off, LANES), width)
            flying[g] = go([
                copy(g, 0, part_ref.at[:, theirs], core_in.at[:, pl.ds(off, width)], core_peer)
            ])

    def use(pair, side):
        cols = pair_cols(pair, side)
        dec_grad_ref[:, cols] = (
            jnp.dot(turned_ref[...], out_ref[:, cols], preferred_element_type=jnp.float32) * factor
        )

        def add(i):
            rows = pl.ds(i, own_tokens)
            back_prop[rows, :] += contract_last(out_ref[rows, cols], dec_ref[:, cols])

        by_rows(tokens, own_tokens, add)

    make(0)
    back_prop[...] = jnp.zeros_like(back_prop)
    make(1)

    def sum_cores(g):
        off, width = groups[g]
        b1, b2, p1, p2 = bits(g)
        cols, own = pl.ds(off, width), mine(off, width)

        def add(i):
            rows = pl.ds(i, own_tokens)
            acc0[rows, cols] = (term(i, own) + core_in[rows, cols].astype(jnp.float32)).astype(
                jnp.bfloat16
            )

        by_rows(tokens, own_tokens, add)
        return [copy(g, 1, acc0.at[rows_at((1 - b1) * t1, t1), cols], in1.at[:, cols], p1)]

    def sum_first(g):
        off, width = groups[g]
        b1, b2, p1, p2 = bits(g)
        cols = pl.ds(off, width)

        def add(i):
            kept = pl.ds(pl.multiple_of(b1 * t1 + i, 128), 128)
            rows = pl.ds(i, 128)
            acc1[rows, cols] = (
                acc0[kept, cols].astype(jnp.float32) + in1[rows, cols].astype(jnp.float32)
            ).astype(jnp.bfloat16)

        by_rows(t1, 128, add)
        return [copy(g, 2, acc1.at[rows_at((1 - b2) * t2, t2), cols], in2.at[:, cols], p2)]

    def sum_second(g):
        off, width = groups[g]
        b1, b2, p1, p2 = bits(g)
        cols = pl.ds(off, width)

        def add(i):
            kept = pl.ds(pl.multiple_of(b2 * t2 + i, 128), 128)
            rows = pl.ds(i, 128)
            acc2[rows, cols] = (
                acc1[kept, cols].astype(jnp.float32) + in2[rows, cols].astype(jnp.float32)
            ).astype(jnp.bfloat16)

        by_rows(t2, 128, add)
        return [
            copy(g, 3 + d, acc2.at[rows_at(lax.rem(z + 1 + d, z_size) * t3, t3), cols],
                 in3.at[d, :, cols], z_peers[d])
            for d in range(z_size - 1)
        ]

    def sum_last(g):
        off, width = groups[g]
        b1, b2, p1, p2 = bits(g)
        cols, own = pl.ds(off, width), mine(off, width)
        start = b1 * t1 + b2 * t2 + z * t3
        total = acc2[rows_at(z * t3, t3), cols].astype(jnp.float32)
        for d in range(z_size - 1):
            total = total + in3[d, :, cols].astype(jnp.float32)
        out_ref[rows_at(start, t3), own] = (total + bias_ref[:, own]).astype(jnp.bfloat16)
        block = out_ref.at[rows_at(start, t3), own]
        return [copy(g, base + d, block, block, z_peers[d]) for d in range(z_size - 1)]

    def give_quarter(g):
        b1, b2, p1, p2 = bits(g)
        block = out_ref.at[rows_at(b1 * t1 + b2 * t2, t2), mine(*groups[g])]
        return [copy(g, base + z_size - 1, block, block, p2)]

    def give_half(g):
        b1, b2, p1, p2 = bits(g)
        block = out_ref.at[rows_at(b1 * t1, t1), mine(*groups[g])]
        return [copy(g, base + z_size, block, block, p1)]

    def give_core(g):
        block = out_ref.at[:, mine(*groups[g])]
        return [copy(g, base + z_size + 1, block, block, core_peer)]

    def end(g):
        return []

    work = (sum_cores, sum_first, sum_second, sum_last, give_quarter, give_half, give_core, end)
    pairs = (count + 1) // 2
    for step in range(pairs + LAGS[-1]):
        for stage in (0,) + tuple(range(len(work) - 1, 0, -1)):
            pair = step - LAGS[stage]
            for g in (2 * pair, 2 * pair + 1):
                if 0 <= g < count:
                    for c in flying[g]:
                        c.wait_recv()
                    flying[g] = go(work[stage](g))
        make(step + 2)
        for stage, side in ((6, core), (7, 1 - core)):
            if 0 <= step - LAGS[stage] < pairs:
                use(step - LAGS[stage], side)

    def slopes(i):
        rows = pl.ds(i, own_tokens)
        slope_ref[rows, :] = (back_prop[rows, :] * 2.0 * rect_ref[rows, :]).astype(jnp.bfloat16)

    by_rows(tokens, own_tokens, slopes)
    for c in started:
        c.wait_send()


def total_and_grads(latent, rect, w_dec, target, bias, z_size, factor):
    tokens, own_latents = latent.shape
    features = w_dec.shape[1]
    half_f = features // 2
    stages = 2 * (3 + z_size - 1) * len(groups_of(half_f))
    t1, t2, t3 = tokens // 2, tokens // 4, tokens // (4 * z_size)
    bf = jnp.bfloat16
    return pl.pallas_call(
        functools.partial(total_kernel, z_size, factor),
        out_shape=(
            jax.ShapeDtypeStruct((own_latents, features), jnp.float32),
            jax.ShapeDtypeStruct((tokens, own_latents), bf),
        ),
        in_specs=[pl.BlockSpec(memory_space=pltpu.VMEM)] * 6,
        out_specs=(pl.BlockSpec(memory_space=pltpu.VMEM),) * 2,
        scratch_shapes=[
            pltpu.VMEM((tokens, features), bf),
            pltpu.VMEM((tokens, features), bf),
            pltpu.VMEM((tokens, own_latents), jnp.float32),
            pltpu.VMEM((tokens, half_f), bf),
            pltpu.VMEM((tokens, half_f), bf),
            pltpu.VMEM((t1, half_f), bf),
            pltpu.VMEM((t1, half_f), bf),
            pltpu.VMEM((t2, half_f), bf),
            pltpu.VMEM((t2, half_f), bf),
            pltpu.VMEM((z_size - 1, t3, half_f), bf),
            pltpu.SemaphoreType.DMA((stages,)),
            pltpu.SemaphoreType.DMA((stages,)),
        ],
        compiler_params=pltpu.CompilerParams(
            collective_id=0, has_side_effects=True, vmem_limit_bytes=44 * 1024 * 1024
        ),
    )(latent, latent.T, rect, w_dec, target, bias)


PIECES = 4


def widest(size, options):
    return next(w for w in options if size % w == 0)


def mlp_kernel(
    own_ref, gate_ref, up_ref, down_ref, tok_ref, target_ref,
    hidden, gates, ups, downs, load_sem, own_sem, send_sem, recv_sem,
):
    count, features = own_ref.shape
    row, hid = lax.axis_index("rows"), lax.axis_index("hidden")
    x, core, z, y = row // 2, row % 2, hid // 2, hid % 2
    across = (1 - x) * 2 + core
    core_peer = {"rows": x * 2 + (1 - core), "hidden": hid}
    x_peer = {"rows": across, "hidden": hid}
    y_peer = {"rows": row, "hidden": z * 2 + (1 - y)}
    barrier = pltpu.get_barrier_semaphore()
    for peer in (core_peer, x_peer, y_peer):
        pl.semaphore_signal(barrier, inc=1, device_id=peer, device_id_type=pl.DeviceIdType.MESH)
    pl.semaphore_wait(barrier, 3)

    half = count // 2
    size = half // PIECES

    def copy(at, src, dst, peer):
        return pltpu.make_async_remote_copy(
            src_ref=src, dst_ref=dst, send_sem=send_sem.at[at], recv_sem=recv_sem.at[at],
            device_id=peer, device_id_type=pl.DeviceIdType.MESH,
        )

    def tok(start, rows):
        return tok_ref.at[pl.ds(pl.multiple_of(start, rows), rows), :]

    mine = tok(row * count, count)
    place = pltpu.make_async_copy(own_ref, mine, own_sem)
    to_core = copy(0, own_ref, mine, core_peer)
    over_x, over_y, core_x, core_y = [], [], [], []
    for i in range(PIECES):
        here = y * half + i * size
        there = (1 - y) * half + i * size
        piece = own_ref.at[pl.ds(pl.multiple_of(here, size), size), :]
        over_x.append(copy(1 + i, piece, tok(row * count + here, size), x_peer))
        got = tok(across * count + here, size)
        far = tok(across * count + there, size)
        over_y.append(copy(1 + PIECES + i, got, got, y_peer))
        core_x.append(copy(1 + 2 * PIECES + i, got, got, core_peer))
        core_y.append(copy(1 + 3 * PIECES + i, far, far, core_peer))

    for c in over_x:
        c.start()
    to_core.start()
    place.start()

    def took_x(i):
        over_x[i].wait_recv()
        over_y[i].start()
        core_x[i].start()

    def took_y(i):
        over_y[i].wait_recv()
        core_y[i].start()

    width, down_width = gates.shape[2], downs.shape[2]
    steps, down_steps = gate_ref.shape[1] // width, features // down_width

    def tile(i, width, count):
        return pl.ds(0 if count == 1 else pl.multiple_of(i * width, width), width)

    def loads(i):
        slot = lax.rem(i, 2)
        cols = tile(i, width, steps)
        return (
            pltpu.make_async_copy(gate_ref.at[:, cols], gates.at[slot], load_sem.at[slot]),
            pltpu.make_async_copy(up_ref.at[:, cols], ups.at[slot], load_sem.at[2 + slot]),
        )

    def down_loads(i):
        slot = lax.rem(i, 2)
        cols = pl.ds(pl.multiple_of(i * down_width, down_width), down_width)
        return (pltpu.make_async_copy(down_ref.at[:, cols], downs.at[slot], load_sem.at[4 + slot]),)

    def start(copies):
        for c in copies:
            c.start()

    def gate_step(i, carry):
        @pl.when(i + 1 < steps)
        def _():
            start(loads(i + 1))

        for c in loads(i):
            c.wait()
        slot = lax.rem(i, 2)
        gate = jnp.dot(own_ref[...], gates[slot], preferred_element_type=jnp.float32)
        up = jnp.dot(own_ref[...], ups[slot], preferred_element_type=jnp.float32)
        hidden[:, tile(i, width, steps)] = (
            jax.nn.gelu(gate, approximate=True) * up
        ).astype(jnp.bfloat16)
        return carry

    def down_step(i, carry):
        @pl.when(i + 1 < down_steps)
        def _():
            start(down_loads(i + 1))

        for c in down_loads(i):
            c.wait()
        target_ref[:, pl.ds(pl.multiple_of(i * down_width, down_width), down_width)] = jnp.dot(
            hidden[...], downs[lax.rem(i, 2)], preferred_element_type=jnp.float32
        )
        return carry

    start(loads(0))
    start(down_loads(0))
    done = 0
    for i in range(PIECES):
        until = min(steps, 2 * (i + 1))
        lax.fori_loop(done, until, gate_step, 0)
        done = until
        took_x(i)
        if i:
            took_y(i - 1)
    lax.fori_loop(done, steps, gate_step, 0)
    middle = (down_steps * 2) // 3
    lax.fori_loop(0, middle, down_step, 0)
    took_y(PIECES - 1)
    lax.fori_loop(middle, down_steps, down_step, 0)

    place.wait()
    to_core.wait_recv()
    for c in core_x + core_y:
        c.wait_recv()
    for c in [to_core] + over_x + over_y + core_x + core_y:
        c.wait_send()


def gather_and_mlp(own, w_gate, w_up, w_down):
    count, features = own.shape
    units = w_gate.shape[1]
    width = widest(units, (256, 128, units))
    down_width = widest(features, (512, 256, 128))
    bf = jnp.bfloat16
    copies = 1 + 4 * PIECES
    vmem, anywhere = pl.BlockSpec(memory_space=pltpu.VMEM), pl.BlockSpec(memory_space=pl.ANY)
    return pl.pallas_call(
        mlp_kernel,
        out_shape=(
            jax.ShapeDtypeStruct((lax.axis_size("rows") * count, features), bf),
            jax.ShapeDtypeStruct((count, features), jnp.float32),
        ),
        in_specs=[vmem, anywhere, anywhere, anywhere],
        out_specs=(vmem, vmem),
        scratch_shapes=[
            pltpu.VMEM((count, units), bf),
            pltpu.VMEM((2, features, width), bf),
            pltpu.VMEM((2, features, width), bf),
            pltpu.VMEM((2, units, down_width), bf),
            pltpu.SemaphoreType.DMA((6,)),
            pltpu.SemaphoreType.DMA,
            pltpu.SemaphoreType.DMA((copies,)),
            pltpu.SemaphoreType.DMA((copies,)),
        ],
        compiler_params=pltpu.CompilerParams(
            collective_id=1, has_side_effects=True, vmem_limit_bytes=48 * 1024 * 1024
        ),
    )(own, w_gate, w_up, w_down)


def on_device(z_size, resid_stream, pre_gain, w_gate, w_up, w_down, w_enc, b_enc, w_dec, b_dec):
    normal_in = normed(resid_stream, pre_gain)
    tok_rows, target = gather_and_mlp(normal_in, w_gate, w_up, w_down)
    row_size = lax.axis_size("rows")
    own_tokens, features = normal_in.shape
    factor = 1.0 / math.sqrt(own_tokens * row_size)
    own_pre = jnp.dot(tok_rows, w_enc, preferred_element_type=jnp.float32) + b_enc.astype(
        jnp.float32
    )
    own_rect = jnp.maximum(own_pre, 0.0)
    own_latent = (own_rect * own_rect).astype(jnp.bfloat16)
    dec_grad, own_slope = total_and_grads(
        own_latent, own_rect, w_dec, target, b_dec.reshape(1, features), z_size, factor
    )
    return (contract_first(tok_rows, own_slope) * factor, dec_grad)


def solution(mesh):
    return jax.shard_map(
        functools.partial(on_device, mesh.shape["hidden"] // 2),
        mesh=mesh,
        in_specs=(
            P("rows", None),
            P(),
            P(None, "hidden"),
            P(None, "hidden"),
            P("hidden", None),
            P(None, ("rows", "hidden")),
            P(("rows", "hidden")),
            P(("rows", "hidden"), None),
            P(),
        ),
        out_specs=(P(None, ("rows", "hidden")), P(("rows", "hidden"), None)),
        check_vma=False,
    )
```
